32 devices in a mesh: seq: 16 (over z, x, core), chan: 2 (over y).
Axes of the slice: x: 2, y: 2, z: 4, core: 2. Of those that a mesh axis runs over, the one named last changes fastest.
Arguments:
- loaded: bfloat16 [3, 16384, 4096], P(None, 'seq', 'chan'), may hold values from -6 to 6
- dest_tiles: int32 [512], P('seq'), may hold values from 0 to 255, as said below
- tile_counts: int32 [16], P('seq'), may hold values from 8 to 32, as said below
- segments: int32 [8192], P('seq'), may hold values from 0 to 31, never falling along the last dimension, each value on 1 to 1024 neighbouring positions
- short_filters: float32 [3, 7, 4096], P(None, None, 'chan')
- long_filters: bfloat16 [256, 8192], P('chan', 'seq')
- skip_gain: float32 [4096], P('chan'), may hold values from 0.5 to 1.5
- norm_gain: float32 [4096], P('chan'), may hold values from 0.5 to 1.5
Outputs:
- layer_out: bfloat16 [8192, 4096], P('seq', 'chan')
The draws below stay inside these ranges and needn't reach their ends.
Inputs may be any that keep to these rules, and one draw needn't show every extreme that they name: Index s of seq holds tile_counts[s] tiles in its first slots; the busiest holds exactly 32, and every count is a multiple of 4. `dest_tiles`: entry s * 32 + j names the tile held in slot j of index s when j < tile_counts[s]; later slots name arbitrary tiles. The used slots name every tile exactly once. Tile d belongs to index d // 16 of seq, and one index holds either none or exactly 4 tiles of any one index.
All inputs are finite; a program needn't handle non-finite values.
Results may differ from the reference program's by a relative error of at most 0.0057.
Values may be sent and summed in bfloat16 or wider, within the bound.
A program may use at most 192 MiB of HBM per device.

```python
import math
import jax
import jax.numpy as jnp
import numpy as np
from jax import lax

CHANNELS = 4096
GROUP_SIZE = 16
SHORT = 7
TILE = 32
TILES_DEV = 16
PACKED_TOKENS = 8192
NTILES = 256
CAP = 32
LONG_FILTER_SET = 256
DOCS = 32
N_SEQ = 16


def route_tables(key):
    devices = N_SEQ
    per_device = TILES_DEV
    pair_count = 4 * per_device // devices
    slot_count = 2 * per_device
    repeats = np.array([devices // 2, devices // 4, devices // 8, devices // 8] * (devices // 4))
    entry_total = devices * devices // 4
    entry_dst = np.arange(entry_total) % devices
    entry_rank = np.arange(entry_total) // devices
    random_subkeys = jax.random.split(jax.random.fold_in(key, 11), 5)
    src_perm = jax.random.permutation(random_subkeys[0], devices)
    dst_perm = jax.random.permutation(random_subkeys[1], devices)
    local_perm = jax.vmap(lambda sub: jax.random.permutation(sub, per_device))(jax.random.split(random_subkeys[2], devices))
    within = entry_rank[:, None] * pair_count + np.arange(pair_count)[None, :]
    tile_ids = dst_perm[entry_dst][:, None] * per_device + local_perm[entry_dst[:, None], within]
    starts = np.concatenate([[0], np.cumsum(repeats)[:-1]])
    counts_pre = repeats * pair_count
    slot_rows = []
    for source in range(devices):
        used = int(counts_pre[source])
        run_tiles = tile_ids[int(starts[source]):int(starts[source]) + int(repeats[source])].reshape(-1)
        shuffle = jax.random.permutation(jax.random.fold_in(random_subkeys[3], source), used)
        filler = jax.random.randint(jax.random.fold_in(random_subkeys[4], source), (slot_count - used,), 0, devices * per_device)
        slot_rows.append(jnp.concatenate([run_tiles[shuffle], filler]))
    slot_table = jnp.stack(slot_rows)
    inverse = jnp.argsort(src_perm)
    dest_list = slot_table[inverse].reshape(-1).astype(jnp.int32)
    count_list = jnp.asarray(counts_pre, jnp.int32)[inverse]
    return (dest_list, count_list)


def draw_dest_tiles(key, part):
    return route_tables(key)[0]


def draw_tile_counts(key, part):
    return route_tables(key)[1]


def draw_short_filters(key, part):
    random_subkeys = jax.random.split(jax.random.fold_in(key, 3), 2)
    filter_jitter = jax.random.normal(random_subkeys[0], (3, SHORT, CHANNELS))
    ramp_power = 0.5
    spread = jnp.exp(0.5 * jax.random.uniform(random_subkeys[1], (CHANNELS,), minval=0.0, maxval=math.log(10.0)))
    channel_ramp = jnp.exp(ramp_power * math.log(3.0) * jnp.arange(CHANNELS, dtype=jnp.float32) / (CHANNELS - 1))
    row_scale = jnp.stack([spread * channel_ramp, jnp.ones((CHANNELS,), jnp.float32), jnp.ones((CHANNELS,), jnp.float32)])
    return (filter_jitter * row_scale[:, None, :] / math.sqrt(SHORT)).astype(jnp.float32)


def unit_power(rate):
    return jnp.expm1(-2.0 * rate * PACKED_TOKENS) / jnp.expm1(-2.0 * rate)


def draw_long_filters(key, part):
    random_subkeys = jax.random.split(jax.random.fold_in(key, 5), 8)
    delay_index = jnp.arange(PACKED_TOKENS, dtype=jnp.float32)[None, :]
    fast_share = 0.5
    filter_jitter = jax.random.normal(random_subkeys[0], (LONG_FILTER_SET, PACKED_TOKENS))
    second_jitter = jax.random.normal(random_subkeys[5], (LONG_FILTER_SET, PACKED_TOKENS))
    fast_filter = jax.random.uniform(random_subkeys[1], (LONG_FILTER_SET, 1)) < fast_share
    fast_rate = jax.random.uniform(random_subkeys[2], (LONG_FILTER_SET, 1), minval=1.0 / 50, maxval=1.0 / 30)
    slow_rate = jax.random.uniform(random_subkeys[3], (LONG_FILTER_SET, 1), minval=0.1, maxval=1.0) / PACKED_TOKENS
    falloff_speed = jnp.where(fast_filter, fast_rate, slow_rate)
    second_rate = jax.random.uniform(random_subkeys[6], (LONG_FILTER_SET, 1), minval=0.1, maxval=1.0) / PACKED_TOKENS
    second_share = jnp.where(fast_filter, jax.random.uniform(random_subkeys[7], (LONG_FILTER_SET, 1), minval=0.05, maxval=0.15), 0.0)
    spike_position = jax.random.uniform(random_subkeys[4], (LONG_FILTER_SET, 2), minval=0.05, maxval=0.95) * PACKED_TOKENS
    spike_penalty = jnp.where(delay_index >= spike_position[:, 0:1], 0.7, 1.0) * jnp.where(delay_index >= spike_position[:, 1:2], 0.7, 1.0)
    first_part = filter_jitter * jnp.exp(-falloff_speed * delay_index) / jnp.sqrt(unit_power(falloff_speed))
    second_part = second_jitter * jnp.exp(-second_rate * delay_index) / jnp.sqrt(unit_power(second_rate))
    value_entries = (jnp.sqrt(1.0 - second_share) * first_part + jnp.sqrt(second_share) * second_part) * spike_penalty
    return value_entries.astype(jnp.bfloat16)


def block_scale(rng, shape, cuts, least, largest):
    def one(dim, shards_of):
        draws = jax.random.uniform(jax.random.fold_in(jax.random.fold_in(rng, 6), dim), (shards_of,), jnp.float32, least / len(cuts), largest / len(cuts))
        return jnp.repeat(jnp.exp(draws), shape[dim] // shards_of).reshape((-1,) + (1,) * (len(shape) - dim - 1))

    level = one(*cuts[0])
    for cut in cuts[1:]:
        level = level * one(*cut)
    return level


def split_up(number_of, total, limit, lean):
    loads = [(1 << 20) // math.isqrt(rank ** lean) + 1 for rank in range(2, number_of + 1)]
    surplus, holding = total - limit - (number_of - 1), [1] * (number_of - 1)
    while surplus > 0:
        candidates = [i for i in range(number_of - 1) if holding[i] < limit]
        whole, left = sum([loads[i] for i in candidates]), surplus
        for i in candidates:
            more = min(limit - holding[i], max(1, left * loads[i] // whole), surplus)
            holding[i] = holding[i] + more
            surplus = surplus - more
    return np.array([limit] + holding)


def uneven_parts(rng, count, total, bound, lean):
    if count == 2:
        one = jax.random.randint(rng, (), max(1, total - bound), min(bound, total - 1) + 1)
        return jnp.stack([one, total - one])
    sizes = jnp.asarray(split_up(count, total, bound, lean), jnp.int32)
    twos = (count - 1) // 2
    source_of, receiver = sizes[1:1 + 2 * twos:2], sizes[2:2 + 2 * twos:2]
    slack = jnp.minimum(source_of - 1, bound - receiver)
    shifted = jax.random.randint(jax.random.fold_in(rng, 1), (twos,), 0, 1 << 20) % (slack + 1)
    sizes = sizes.at[1:1 + 2 * twos:2].set(source_of - shifted).at[2:2 + 2 * twos:2].set(receiver + shifted)
    return sizes[jax.random.permutation(jax.random.fold_in(rng, 2), count)]


def scatter_about(stream_key, shape, scale, bound, pieces=(), kind=jnp.bfloat16):
    level = block_scale(stream_key, shape, pieces, -0.22, 0.18) if pieces else 1.0
    result = jax.random.normal(stream_key, shape, jnp.float32) * scale * level
    return jnp.minimum(jnp.maximum(result, -bound), bound).astype(kind)


def setup_inputs(seed: int = 0) -> dict:
    seeds = jax.random.split(jax.random.key(seed), 9)
    return {
        "loaded": scatter_about(seeds[0], (3, N_SEQ * CAP * TILE, CHANNELS), 1.0, 6.0, ((1, 16), (2, 2))),
        "dest_tiles": draw_dest_tiles(jax.random.fold_in(seeds[8], 71), 0),
        "tile_counts": draw_tile_counts(jax.random.fold_in(seeds[8], 71), 0),
        "segments": jnp.searchsorted(jnp.cumsum(uneven_parts(seeds[3], DOCS, PACKED_TOKENS, min(1024, PACKED_TOKENS - DOCS + 1), 2)), jnp.arange(PACKED_TOKENS), side="right").astype(jnp.int32),
        "short_filters": draw_short_filters(jax.random.fold_in(seeds[8], 71), 0),
        "long_filters": draw_long_filters(jax.random.fold_in(seeds[8], 71), 0),
        "skip_gain": jnp.clip(0.5 + 1.0 * jax.random.uniform(seeds[6], (CHANNELS,), jnp.float32) ** block_scale(seeds[6], (CHANNELS,), ((0, 2),), -0.2, 0.2), 0.5, 1.5),
        "norm_gain": jnp.clip(1.0 + 0.1 * jax.random.normal(seeds[7], (CHANNELS,), jnp.float32), 0.5, 1.5),
    }


def reference(loaded, dest_tiles, tile_counts, segments, short_filters, long_filters, skip_gain, norm_gain):
    slot_total = N_SEQ * CAP
    slot_ids = jnp.arange(slot_total, dtype=jnp.int32)
    valid_slot = slot_ids % CAP < jnp.repeat(tile_counts, CAP)
    target = jnp.where(valid_slot, dest_tiles, NTILES).astype(jnp.int32)
    holder = jnp.zeros((NTILES,), jnp.int32).at[target].set(slot_ids, mode='drop')
    same_doc = []
    for offset in range(SHORT):
        head_rows = jnp.zeros((offset,), jnp.bool_)
        same_doc.append(jnp.concatenate([head_rows, segments[offset:] == segments[:PACKED_TOKENS - offset]]))

    def one_group(group_index):
        first_column = group_index * GROUP_SIZE
        columns = lax.dynamic_slice_in_dim(loaded, first_column, GROUP_SIZE, 2)
        tile_blocks = columns.reshape(3, slot_total, TILE, GROUP_SIZE)
        arranged = jnp.take(tile_blocks, holder, axis=1).reshape(3, PACKED_TOKENS, GROUP_SIZE).astype(jnp.float32)
        tap_weights = lax.dynamic_slice_in_dim(short_filters, first_column, GROUP_SIZE, 2)
        filtered = jnp.zeros((3, PACKED_TOKENS, GROUP_SIZE), jnp.float32)
        for offset in range(SHORT):
            delayed = jnp.pad(arranged[:, :PACKED_TOKENS - offset], ((0, 0), (offset, 0), (0, 0)))
            filtered = filtered + jnp.where(same_doc[offset][None, :, None], delayed, 0.0) * tap_weights[:, offset][:, None, :]
        gate_rows = lax.optimization_barrier(filtered[0].astype(jnp.bfloat16)).astype(jnp.float32)
        mixed_rows = lax.optimization_barrier((filtered[1] * filtered[2]).astype(jnp.bfloat16)).astype(jnp.float32)
        kernel = lax.dynamic_index_in_dim(long_filters, group_index, 0, keepdims=False).astype(jnp.float32)
        spectrum = jnp.fft.rfft(mixed_rows, n=2 * PACKED_TOKENS, axis=0) * jnp.fft.rfft(kernel, n=2 * PACKED_TOKENS)[:, None]
        convolved = jnp.fft.irfft(spectrum, n=2 * PACKED_TOKENS, axis=0)[:PACKED_TOKENS]
        direct = lax.dynamic_slice_in_dim(skip_gain, first_column, GROUP_SIZE, 0)
        return gate_rows * (convolved + direct[None, :] * mixed_rows)
    gated_rows = lax.map(one_group, jnp.arange(LONG_FILTER_SET, dtype=jnp.int32))
    gated_rows = jnp.transpose(gated_rows, (1, 0, 2)).reshape(PACKED_TOKENS, CHANNELS)
    row_power = lax.optimization_barrier(jnp.mean(gated_rows * gated_rows, axis=1))
    return (gated_rows * lax.rsqrt(row_power + 1e-06)[:, None] * norm_gain[None, :]).astype(jnp.bfloat16)
```

```python
import functools

import jax
import jax.numpy as jnp
from jax import lax
from jax.experimental import pallas as pl
from jax.experimental.pallas import tpu as pltpu
from jax.sharding import PartitionSpec as P

GROUP_SIZE = 16
TILE = 32
BLOCK = 256
LANES = 128
CHUNK = 1024


def place_and_filter(holder, recv, reach, taps, gate, mixed, cap, rows_r, tile):
    slot = holder[tile]
    back = holder[jnp.maximum(tile - 1, 0)]
    start = pl.multiple_of(lax.rem(slot, cap) * TILE, TILE)
    back_start = pl.multiple_of(lax.rem(back, cap) * TILE + TILE // 2, TILE // 2)
    source, back_source = slot // cap, back // cap
    row = pl.multiple_of(tile * TILE, TILE)
    limit = reach[pl.ds(row, TILE), :].astype(jnp.float32)
    results = []
    for r in rows_r:
        here = recv[source, r, pl.ds(start, TILE), :].astype(jnp.float32)
        before = recv[back_source, r, pl.ds(back_start, TILE // 2), :].astype(jnp.float32)
        ext = jnp.concatenate([before[TILE // 2 - 8 :], here], axis=0)
        total = here * taps[r, 0:1, :]
        for offset in range(1, 7):
            window = ext[8 - offset : 8 - offset + TILE]
            total = total + jnp.where(limit >= offset, window, 0.0) * taps[r, offset : offset + 1, :]
        results.append(total)
    return row, results


def long_conv(bands, toep, xt, yt, groups, blocks):
    seq = blocks * BLOCK
    toep[LANES:, 0:LANES] = jnp.zeros((LANES, LANES), toep.dtype)

    @pl.loop(0, groups)
    def _(g):
        @pl.loop(0, seq // CHUNK)
        def _(c):
            base = pl.multiple_of(c * CHUNK, CHUNK)
            part = bands[g, :, pl.ds(base, CHUNK + LANES)].astype(jnp.float32)
            for k in range(8):
                rolled = part if k == 0 else pltpu.roll(part, 16 * k, 1)
                rolled = rolled[:, LANES:].astype(toep.dtype)
                toep[16 * k : 16 * k + 16, pl.ds(base, CHUNK)] = rolled
                toep[LANES + 16 * k : LANES + 16 * k + 16, pl.ds(base + LANES, CHUNK)] = rolled

        yt[g] = jnp.zeros((blocks * GROUP_SIZE, BLOCK), jnp.float32)
        stages = 4
        for stage in range(stages):
            first = stage * blocks // stages
            rows = (blocks - first) * GROUP_SIZE

            @pl.loop(first, first + blocks // stages)
            def _(d):
                begin = pl.multiple_of(
                    (blocks + first - d) * GROUP_SIZE, GROUP_SIZE
                )
                lags = pl.multiple_of(d * BLOCK, BLOCK)
                yt[g, first * GROUP_SIZE :, :] += jnp.dot(
                    xt[g, pl.ds(begin, rows), :],
                    toep[:, pl.ds(lags, BLOCK)],
                    preferred_element_type=jnp.float32,
                )


def to_columns(mixed, xt, groups, block, blocks):
    row = pl.multiple_of(block * BLOCK, BLOCK)
    turned = mixed[pl.ds(row, BLOCK), :].astype(jnp.float32).T.astype(jnp.bfloat16)
    at = pl.multiple_of((blocks + block) * GROUP_SIZE, GROUP_SIZE)
    for g in range(groups):
        xt[g, pl.ds(at, GROUP_SIZE), :] = turned[g * GROUP_SIZE : (g + 1) * GROUP_SIZE]


def gate_block(gate, mixed, yt, skip, groups, block):
    row = pl.multiple_of(block * BLOCK, BLOCK)
    at = pl.multiple_of(block * GROUP_SIZE, GROUP_SIZE)
    parts = [yt[g, pl.ds(at, GROUP_SIZE), :] for g in range(groups)]
    if groups * GROUP_SIZE < LANES:
        parts.append(jnp.zeros((LANES - groups * GROUP_SIZE, BLOCK), jnp.float32))
    convolved = jnp.concatenate(parts, axis=0).T
    return gate[pl.ds(row, BLOCK), :].astype(jnp.float32) * (
        convolved + skip[...] * mixed[pl.ds(row, BLOCK), :].astype(jnp.float32)
    )


def operator_kernel(
    cap, groups, blocks, holder, recv, reach, taps, skip, bands, out, gate, mixed, xt, yt, toep
):
    tiles = BLOCK // TILE
    for g in range(groups):
        xt[g, 0 : blocks * GROUP_SIZE, :] = jnp.zeros((blocks * GROUP_SIZE, BLOCK), xt.dtype)

    @pl.loop(0, blocks)
    def _(block):
        @pl.loop(0, tiles)
        def _(i):
            row, (q, k, v) = place_and_filter(
                holder, recv, reach, taps, gate, mixed, cap, (0, 1, 2), block * tiles + i
            )
            gate[pl.ds(row, TILE), :] = q.astype(jnp.bfloat16)
            mixed[pl.ds(row, TILE), :] = (k * v).astype(jnp.bfloat16)

        to_columns(mixed, xt, groups, block, blocks)

    long_conv(bands, toep, xt, yt, groups, blocks)

    @pl.loop(0, blocks)
    def _(block):
        row = pl.multiple_of(block * BLOCK, BLOCK)
        out[pl.ds(row, BLOCK), :] = gate_block(gate, mixed, yt, skip, groups, block).astype(
            jnp.bfloat16
        )


def operator(holder, recv, reach, taps, skip, bands, cap, groups):
    seq = reach.shape[0]
    blocks = seq // BLOCK
    vmem = pl.BlockSpec(memory_space=pltpu.VMEM)
    return pl.pallas_call(
        functools.partial(operator_kernel, cap, groups, blocks),
        out_shape=jax.ShapeDtypeStruct((seq, LANES), jnp.bfloat16),
        in_specs=[pl.BlockSpec(memory_space=pltpu.SMEM)] + [vmem] * 5,
        out_specs=vmem,
        scratch_shapes=[
            pltpu.VMEM((seq, LANES), jnp.bfloat16),
            pltpu.VMEM((seq, LANES), jnp.bfloat16),
            pltpu.VMEM((groups, 2 * blocks * GROUP_SIZE, BLOCK), jnp.bfloat16),
            pltpu.VMEM((groups, blocks * GROUP_SIZE, BLOCK), jnp.float32),
            pltpu.VMEM((BLOCK, seq + LANES), jnp.bfloat16),
        ],
        compiler_params=pltpu.CompilerParams(vmem_limit_bytes=62 * 2**20),
    )(holder, recv, reach, taps, skip, bands)


def routing(dest_tiles, tile_counts, segments):
    cap = dest_tiles.shape[0]
    slots = lax.all_gather(dest_tiles, "seq", tiled=True)
    counts = lax.all_gather(tile_counts, "seq", tiled=True)
    docs = lax.all_gather(segments, "seq", tiled=True)
    seq = docs.shape[0]
    ids = jnp.arange(slots.shape[0], dtype=jnp.int32)
    used = ids % cap < jnp.repeat(counts, cap)
    hits = (slots[None, :] == jnp.arange(seq // TILE, dtype=jnp.int32)[:, None]) & used[None, :]
    holder = jnp.sum(jnp.where(hits, ids[None, :], 0), axis=1)
    reach = jnp.zeros((seq,), jnp.int32)
    for offset in range(1, 7):
        same = docs[offset:] == docs[: seq - offset]
        reach = reach + jnp.pad(same.astype(jnp.int32), (offset, 0))
    return holder, jnp.broadcast_to(reach.astype(jnp.bfloat16)[:, None], (seq, LANES))


def filter_bands(long_filters, devices, groups):
    count, lags = long_filters.shape
    if count < devices * groups:
        long_filters = jnp.repeat(long_filters, devices * groups // count, axis=0)
    mine = lax.all_to_all(long_filters, "seq", split_axis=0, concat_axis=1, tiled=True)
    seq = mine.shape[1]
    padded = jnp.pad(mine, ((0, 0), (LANES, 0)))
    shifted = [padded] + [jnp.pad(padded, ((0, 0), (s, 0)))[:, : seq + LANES] for s in range(1, 16)]
    return jnp.stack(shifted, axis=1)


def local(
    loaded, dest_tiles, tile_counts, segments, short_filters, long_filters, skip_gain, norm_gain
):
    devices = lax.axis_size("seq")
    chans_all = loaded.shape[2] * lax.axis_size("chan")
    chans_here = loaded.shape[2]
    width = chans_here // devices
    groups = max(1, width // GROUP_SIZE)
    rows = loaded.shape[1]
    cap = dest_tiles.shape[0]
    me = lax.axis_index("seq")
    pad = LANES - width
    holder, reach = routing(dest_tiles, tile_counts, segments)
    bands = filter_bands(long_filters, devices, groups)
    taps = lax.dynamic_slice_in_dim(short_filters, me * width, width, 2)
    taps = jnp.pad(taps, ((0, 0), (0, 1), (0, pad)))
    skip = jnp.pad(lax.dynamic_slice_in_dim(skip_gain, me * width, width, 0), (0, pad))[None, :]
    sliced = jnp.transpose(loaded.reshape(3, rows, devices, width), (2, 0, 1, 3))
    recv = lax.all_to_all(sliced, "seq", split_axis=0, concat_axis=0, tiled=True)
    recv = jnp.pad(recv, ((0, 0), (0, 0), (0, 0), (0, pad)))
    gated = operator(holder, recv, reach, taps, skip, bands, cap, groups)[:, :width]
    seq_rows = gated.shape[0] // devices
    back = lax.all_to_all(
        gated.reshape(devices, seq_rows, width), "seq", split_axis=0, concat_axis=0, tiled=True
    )
    gated_rows = jnp.transpose(back, (1, 0, 2)).reshape(seq_rows, chans_here).astype(jnp.float32)
    row_power = lax.psum(jnp.sum(gated_rows * gated_rows, axis=1), "chan") / chans_all
    return (gated_rows * lax.rsqrt(row_power + 1e-06)[:, None] * norm_gain[None, :]).astype(
        jnp.bfloat16
    )


def solution(mesh):
    return jax.shard_map(
        local,
        mesh=mesh,
        in_specs=(
            P(None, "seq", "chan"),
            P("seq"),
            P("seq"),
            P("seq"),
            P(None, None, "chan"),
            P("chan", "seq"),
            P("chan"),
            P("chan"),
        ),
        out_specs=P("seq", "chan"),
        check_vma=False,
    )
```

```python
import functools

import jax
import jax.numpy as jnp
from jax import lax
from jax.experimental import pallas as pl
from jax.experimental.pallas import tpu as pltpu
from jax.sharding import PartitionSpec as P

GROUP_SIZE = 16
TILE = 32
BLOCK = 256
LANES = 128
CHUNK = 1024


def place_and_filter(holder, recv, reach, taps, arrays, first, tile):
    back = jnp.maximum(tile - 1, 0)
    source, slot = holder[0, tile], holder[1, tile]
    back_source, back_slot = holder[0, back], holder[1, back]
    row = pl.multiple_of(tile * TILE, TILE)
    limit = reach[pl.ds(row, TILE), :].astype(jnp.float32)
    results = []
    for r in arrays:
        here = recv[source, r - first, slot, :, :].astype(jnp.float32)
        before = recv[back_source, r - first, back_slot, TILE // 2 :, :].astype(jnp.float32)
        ext = jnp.concatenate([before[TILE // 2 - 8 :], here], axis=0)
        total = here * taps[r, 0:1, :]
        for offset in range(1, 7):
            window = ext[8 - offset : 8 - offset + TILE]
            total = total + jnp.where(limit >= offset, window, 0.0) * taps[r, offset : offset + 1, :]
        results.append(total)
    return row, results


def long_conv(bands, toep, xt, yt, groups, blocks):
    seq = blocks * BLOCK
    toep[LANES:, 0:LANES] = jnp.zeros((LANES, LANES), toep.dtype)

    @pl.loop(0, groups)
    def _(g):
        @pl.loop(0, seq // CHUNK)
        def _(c):
            base = pl.multiple_of(c * CHUNK, CHUNK)
            part = bands[g, :, pl.ds(base, CHUNK + LANES)].astype(jnp.float32)
            for k in range(8):
                rolled = part if k == 0 else pltpu.roll(part, 16 * k, 1)
                rolled = rolled[:, LANES:].astype(toep.dtype)
                toep[16 * k : 16 * k + 16, pl.ds(base, CHUNK)] = rolled
                toep[LANES + 16 * k : LANES + 16 * k + 16, pl.ds(base + LANES, CHUNK)] = rolled

        yt[g] = jnp.zeros((blocks * GROUP_SIZE, BLOCK), jnp.float32)
        stages = 4
        for stage in range(stages):
            first = stage * blocks // stages
            rows = (blocks - first) * GROUP_SIZE

            @pl.loop(first, first + blocks // stages)
            def _(d):
                begin = pl.multiple_of(
                    (blocks + first - d) * GROUP_SIZE, GROUP_SIZE
                )
                lags = pl.multiple_of(d * BLOCK, BLOCK)
                yt[g, first * GROUP_SIZE :, :] += jnp.dot(
                    xt[g, pl.ds(begin, rows), :],
                    toep[:, pl.ds(lags, BLOCK)],
                    preferred_element_type=jnp.float32,
                )


def to_columns(mixed, xt, groups, block, blocks):
    row = pl.multiple_of(block * BLOCK, BLOCK)
    turned = mixed[pl.ds(row, BLOCK), :].astype(jnp.float32).T.astype(jnp.bfloat16)
    at = pl.multiple_of((blocks + block) * GROUP_SIZE, GROUP_SIZE)
    for g in range(groups):
        xt[g, pl.ds(at, GROUP_SIZE), :] = turned[g * GROUP_SIZE : (g + 1) * GROUP_SIZE]


def gate_block(gate, mixed, yt, skip, groups, block):
    row = pl.multiple_of(block * BLOCK, BLOCK)
    at = pl.multiple_of(block * GROUP_SIZE, GROUP_SIZE)
    parts = [yt[g, pl.ds(at, GROUP_SIZE), :] for g in range(groups)]
    if groups * GROUP_SIZE < LANES:
        parts.append(jnp.zeros((LANES - groups * GROUP_SIZE, BLOCK), jnp.float32))
    convolved = jnp.concatenate(parts, axis=0).T
    return gate[pl.ds(row, BLOCK), :].astype(jnp.float32) * (
        convolved + skip[...] * mixed[pl.ds(row, BLOCK), :].astype(jnp.float32)
    )


def operator_kernel(
    groups, blocks, holder, recv, reach, taps, skip, bands, out, gate, mixed, xt, yt, toep
):
    tiles = BLOCK // TILE
    for g in range(groups):
        xt[g, 0 : blocks * GROUP_SIZE, :] = jnp.zeros((blocks * GROUP_SIZE, BLOCK), xt.dtype)

    @pl.loop(0, blocks)
    def _(block):
        @pl.loop(0, tiles)
        def _(i):
            row, (q, k, v) = place_and_filter(
                holder, recv, reach, taps, (0, 1, 2), 0, block * tiles + i
            )
            gate[pl.ds(row, TILE), :] = q.astype(jnp.bfloat16)
            mixed[pl.ds(row, TILE), :] = (k * v).astype(jnp.bfloat16)

        to_columns(mixed, xt, groups, block, blocks)

    long_conv(bands, toep, xt, yt, groups, blocks)

    @pl.loop(0, blocks)
    def _(block):
        row = pl.multiple_of(block * BLOCK, BLOCK)
        out[pl.ds(row, BLOCK), :] = gate_block(gate, mixed, yt, skip, groups, block).astype(
            jnp.bfloat16
        )


def operator(holder, recv, reach, taps, skip, bands, groups):
    seq = reach.shape[0]
    blocks = seq // BLOCK
    vmem = pl.BlockSpec(memory_space=pltpu.VMEM)
    return pl.pallas_call(
        functools.partial(operator_kernel, groups, blocks),
        out_shape=jax.ShapeDtypeStruct((seq, LANES), jnp.bfloat16),
        in_specs=[pl.BlockSpec(memory_space=pltpu.SMEM)] + [vmem] * 5,
        out_specs=vmem,
        scratch_shapes=[
            pltpu.VMEM((seq, LANES), jnp.bfloat16),
            pltpu.VMEM((seq, LANES), jnp.bfloat16),
            pltpu.VMEM((groups, 2 * blocks * GROUP_SIZE, BLOCK), jnp.bfloat16),
            pltpu.VMEM((groups, blocks * GROUP_SIZE, BLOCK), jnp.float32),
            pltpu.VMEM((BLOCK, seq + LANES), jnp.bfloat16),
        ],
        compiler_params=pltpu.CompilerParams(vmem_limit_bytes=62 * 2**20),
    )(holder, recv, reach, taps, skip, bands)


def exchange_kernel(
    blocks, axis_peers, holder, loaded, reach, taps, skip, bands, out,
    recv_q, recv_kv, mixed, xt, yt, toep, gated,
    kv_send, kv_recv, q_send, q_recv, back_send, back_recv, own_sem,
):
    devices = axis_peers
    me = lax.axis_index("seq")
    groups = LANES // GROUP_SIZE
    tiles = BLOCK // TILE
    seq_rows = blocks * BLOCK // devices
    per_device = seq_rows // BLOCK

    def peer_at(k):
        return lax.rem(me + k, devices)

    def lanes_of(index):
        return pl.ds(pl.multiple_of(index * LANES, LANES), LANES)

    def kv_copy(k):
        return pltpu.make_async_remote_copy(
            src_ref=loaded.at[1:3, :, :, lanes_of(peer_at(k))],
            dst_ref=recv_kv.at[me],
            send_sem=kv_send.at[k],
            recv_sem=kv_recv.at[k],
            device_id={"seq": peer_at(k)},
            device_id_type=pl.DeviceIdType.MESH,
        )

    def q_copy(k):
        return pltpu.make_async_remote_copy(
            src_ref=loaded.at[0:1, :, :, lanes_of(peer_at(k))],
            dst_ref=recv_q.at[me],
            send_sem=q_send.at[k],
            recv_sem=q_recv.at[k],
            device_id={"seq": peer_at(k)},
            device_id_type=pl.DeviceIdType.MESH,
        )

    def rows_of(index):
        return pl.ds(pl.multiple_of(index * seq_rows, seq_rows), seq_rows)

    def back_copy(k):
        return pltpu.make_async_remote_copy(
            src_ref=gated.at[rows_of(peer_at(k))],
            dst_ref=out.at[:, lanes_of(me)],
            send_sem=back_send.at[k],
            recv_sem=back_recv.at[k],
            device_id={"seq": peer_at(k)},
            device_id_type=pl.DeviceIdType.MESH,
        )

    barrier = pltpu.get_barrier_semaphore()

    @pl.loop(1, devices)
    def _(k):
        pl.semaphore_signal(
            barrier, inc=1, device_id={"seq": peer_at(k)}, device_id_type=pl.DeviceIdType.MESH
        )

    pl.semaphore_wait(barrier, devices - 1)

    own_kv = pltpu.make_async_copy(
        loaded.at[1:3, :, :, lanes_of(me)], recv_kv.at[me], own_sem.at[0]
    )
    own_q = pltpu.make_async_copy(loaded.at[0:1, :, :, lanes_of(me)], recv_q.at[me], own_sem.at[1])
    own_back = pltpu.make_async_copy(gated.at[rows_of(me)], out.at[:, lanes_of(me)], own_sem.at[2])

    @pl.loop(1, devices)
    def _(k):
        kv_copy(k).start()

    own_kv.start()
    own_q.start()
    for g in range(groups):
        xt[g, 0 : blocks * GROUP_SIZE, :] = jnp.zeros((blocks * GROUP_SIZE, BLOCK), xt.dtype)

    @pl.loop(1, devices)
    def _(k):
        kv_copy(k).wait_send()
        q_copy(k).start()

    own_kv.wait()

    @pl.loop(1, devices)
    def _(k):
        kv_copy(k).wait_recv()

    @pl.loop(0, blocks)
    def _(block):
        @pl.loop(0, tiles)
        def _(i):
            row, (k, v) = place_and_filter(
                holder, recv_kv, reach, taps, (1, 2), 1, block * tiles + i
            )
            mixed[pl.ds(row, TILE), :] = (k * v).astype(jnp.bfloat16)

        to_columns(mixed, xt, groups, block, blocks)

    long_conv(bands, toep, xt, yt, groups, blocks)

    own_q.wait()

    @pl.loop(1, devices)
    def _(k):
        q_copy(k).wait()

    def gate_rows_of(owner):
        for part in range(per_device):
            block = owner * per_device + part

            @pl.loop(0, tiles)
            def _(i):
                row, (q,) = place_and_filter(
                    holder, recv_q, reach, taps, (0,), 0, block * tiles + i
                )
                gated[pl.ds(row, TILE), :] = q.astype(jnp.bfloat16)

            row = pl.multiple_of(block * BLOCK, BLOCK)
            gated[pl.ds(row, BLOCK), :] = gate_block(
                gated, mixed, yt, skip, groups, block
            ).astype(jnp.bfloat16)

    @pl.loop(1, devices)
    def _(k):
        gate_rows_of(peer_at(k))
        back_copy(k).start()

    gate_rows_of(me)
    own_back.start()
    own_back.wait()

    @pl.loop(1, devices)
    def _(k):
        back_copy(k).wait()


def exchange_operator(holder, loaded, reach, taps, skip, bands, devices):
    seq = reach.shape[0]
    blocks = seq // BLOCK
    groups = LANES // GROUP_SIZE
    cap = loaded.shape[1]
    vmem = pl.BlockSpec(memory_space=pltpu.VMEM)
    anywhere = pl.BlockSpec(memory_space=pl.ANY)
    dma = pltpu.SemaphoreType.DMA
    return pl.pallas_call(
        functools.partial(exchange_kernel, blocks, devices),
        out_shape=jax.ShapeDtypeStruct((seq // devices, loaded.shape[3]), jnp.bfloat16),
        in_specs=[pl.BlockSpec(memory_space=pltpu.SMEM), anywhere] + [vmem] * 4,
        out_specs=anywhere,
        scratch_shapes=[
            pltpu.VMEM((devices, 1, cap, TILE, LANES), jnp.bfloat16),
            pltpu.VMEM((devices, 2, cap, TILE, LANES), jnp.bfloat16),
            pltpu.VMEM((seq, LANES), jnp.bfloat16),
            pltpu.VMEM((groups, 2 * blocks * GROUP_SIZE, BLOCK), jnp.bfloat16),
            pltpu.VMEM((groups, blocks * GROUP_SIZE, BLOCK), jnp.float32),
            pltpu.VMEM((BLOCK, seq + LANES), jnp.bfloat16),
            pltpu.VMEM((seq, LANES), jnp.bfloat16),
        ]
        + [dma((devices,))] * 6
        + [dma((3,))],
        compiler_params=pltpu.CompilerParams(
            vmem_limit_bytes=60 * 2**20, collective_id=0, has_side_effects=True
        ),
    )(holder, loaded, reach, taps, skip, bands)


def routing(dest_tiles, tile_counts, segments):
    cap = dest_tiles.shape[0]
    marked = jnp.where(jnp.arange(cap, dtype=jnp.int32) < tile_counts[0], dest_tiles, -1)
    gathered = lax.all_gather(jnp.concatenate([segments, marked]), "seq")
    docs = gathered[:, : segments.shape[0]].reshape(-1)
    slots = gathered[:, segments.shape[0] :].reshape(-1)
    seq = docs.shape[0]
    ids = jnp.arange(slots.shape[0], dtype=jnp.int32)
    hits = slots[None, :] == jnp.arange(seq // TILE, dtype=jnp.int32)[:, None]
    holder = jnp.sum(jnp.where(hits, ids[None, :], 0), axis=1)
    reach = jnp.zeros((seq,), jnp.int32)
    for offset in range(1, 7):
        same = docs[offset:] == docs[: seq - offset]
        reach = reach + jnp.pad(same.astype(jnp.int32), (offset, 0))
    holder = jnp.stack([holder // cap, holder % cap])
    return holder, jnp.broadcast_to(reach.astype(jnp.bfloat16)[:, None], (seq, LANES))


def filter_bands(long_filters, devices, groups):
    count, lags = long_filters.shape
    if count < devices * groups:
        long_filters = jnp.repeat(long_filters, devices * groups // count, axis=0)
    mine = lax.all_to_all(long_filters, "seq", split_axis=0, concat_axis=1, tiled=True)
    seq = mine.shape[1]
    padded = jnp.pad(mine, ((0, 0), (LANES, 0)))
    shifted = [padded] + [jnp.pad(padded, ((0, 0), (s, 0)))[:, : seq + LANES] for s in range(1, 16)]
    return jnp.stack(shifted, axis=1)


def local(
    loaded, dest_tiles, tile_counts, segments, short_filters, long_filters, skip_gain, norm_gain
):
    devices = lax.axis_size("seq")
    chans_all = loaded.shape[2] * lax.axis_size("chan")
    chans_here = loaded.shape[2]
    width = chans_here // devices
    groups = max(1, width // GROUP_SIZE)
    rows = loaded.shape[1]
    cap = dest_tiles.shape[0]
    me = lax.axis_index("seq")
    pad = LANES - width
    holder, reach = routing(dest_tiles, tile_counts, segments)
    bands = filter_bands(long_filters, devices, groups)
    taps = lax.dynamic_slice_in_dim(short_filters, me * width, width, 2)
    taps = jnp.pad(taps, ((0, 0), (0, 1), (0, pad)))
    skip = jnp.pad(lax.dynamic_slice_in_dim(skip_gain, me * width, width, 0), (0, pad))[None, :]
    if width == LANES:
        tiled = loaded.reshape(3, cap, TILE, chans_here)
        arrived = exchange_operator(holder, tiled, reach, taps, skip, bands, devices)
    else:
        sliced = jnp.transpose(loaded.reshape(3, rows, devices, width), (2, 0, 1, 3))
        recv = lax.all_to_all(sliced, "seq", split_axis=0, concat_axis=0, tiled=True)
        recv = jnp.pad(recv, ((0, 0), (0, 0), (0, 0), (0, pad)))
        recv = recv.reshape(devices, 3, cap, TILE, LANES)
        gated = operator(holder, recv, reach, taps, skip, bands, groups)[:, :width]
        seq_rows = gated.shape[0] // devices
        back = lax.all_to_all(
            gated.reshape(devices, seq_rows, width), "seq", split_axis=0, concat_axis=0, tiled=True
        )
        arrived = jnp.transpose(back, (1, 0, 2)).reshape(seq_rows, chans_here)
    gated_rows = arrived.astype(jnp.float32)
    row_power = lax.psum(jnp.sum(gated_rows * gated_rows, axis=1), "chan") / chans_all
    return (gated_rows * lax.rsqrt(row_power + 1e-06)[:, None] * norm_gain[None, :]).astype(
        jnp.bfloat16
    )


def solution(mesh):
    return jax.shard_map(
        local,
        mesh=mesh,
        in_specs=(
            P(None, "seq", "chan"),
            P("seq"),
            P("seq"),
            P("seq"),
            P(None, None, "chan"),
            P("chan", "seq"),
            P("chan"),
            P("chan"),
        ),
        out_specs=P("seq", "chan"),
        check_vma=False,
    )
```

```python
import functools

import jax
import jax.numpy as jnp
from jax import lax
from jax.experimental import pallas as pl
from jax.experimental.pallas import tpu as pltpu
from jax.sharding import PartitionSpec as P

GROUP_SIZE = 16
TILE = 32
BLOCK = 256
LANES = 128
CHUNK = 1024


def place_and_filter(holder, recv, reach, taps, arrays, first, tile):
    back = jnp.maximum(tile - 1, 0)
    source, slot = holder[0, tile], holder[1, tile]
    back_source, back_slot = holder[0, back], holder[1, back]
    row = pl.multiple_of(tile * TILE, TILE)
    limit = reach[pl.ds(row, TILE), :].astype(jnp.float32)
    results = []
    for r in arrays:
        here = recv[source, r - first, slot, :, :].astype(jnp.float32)
        before = recv[back_source, r - first, back_slot, TILE // 2 :, :].astype(jnp.float32)
        ext = jnp.concatenate([before[TILE // 2 - 8 :], here], axis=0)
        total = here * taps[r, 0:1, :]
        for offset in range(1, 7):
            window = ext[8 - offset : 8 - offset + TILE]
            total = total + jnp.where(limit >= offset, window, 0.0) * taps[r, offset : offset + 1, :]
        results.append(total)
    return row, results


def toeplitz(lags, toep, groups, blocks):
    @pl.loop(0, groups)
    def _(g):
        toep[g, :, 0:LANES] = jnp.zeros((LANES, LANES), toep.dtype)

        @pl.loop(0, blocks * BLOCK // CHUNK)
        def _(c):
            base = pl.multiple_of(c * CHUNK, CHUNK)
            part = lags[pl.ds(g, 1), pl.ds(base, CHUNK + LANES)]
            part = jnp.broadcast_to(part, (LANES, CHUNK + LANES))
            rolled = pltpu.roll(part, 0, 1, stride=1, stride_axis=0)
            toep[g, :, pl.ds(base + LANES, CHUNK)] = rolled[:, LANES:].astype(toep.dtype)


def long_conv(toep, xt, yt, groups, blocks):
    @pl.loop(0, groups)
    def _(g):
        yt[g] = jnp.zeros((blocks * GROUP_SIZE, BLOCK), jnp.float32)
        stages = 4
        for stage in range(stages):
            first = stage * blocks // stages
            rows = (blocks - first) * GROUP_SIZE

            @pl.loop(first, first + blocks // stages)
            def _(d):
                begin = pl.multiple_of((blocks + first - d) * GROUP_SIZE, GROUP_SIZE)
                lag = pl.multiple_of(d * BLOCK, BLOCK)
                table = jnp.concatenate(
                    [toep[g, :, pl.ds(lag + LANES, BLOCK)], toep[g, :, pl.ds(lag, BLOCK)]], axis=0
                )
                yt[g, first * GROUP_SIZE :, :] += jnp.dot(
                    xt[g, pl.ds(begin, rows), :], table, preferred_element_type=jnp.float32
                )


def to_columns(mixed, xt, groups, block, blocks):
    row = pl.multiple_of(block * BLOCK, BLOCK)
    turned = mixed[pl.ds(row, BLOCK), :].astype(jnp.float32).T.astype(jnp.bfloat16)
    at = pl.multiple_of((blocks + block) * GROUP_SIZE, GROUP_SIZE)
    for g in range(groups):
        xt[g, pl.ds(at, GROUP_SIZE), :] = turned[g * GROUP_SIZE : (g + 1) * GROUP_SIZE]


def gate_block(gate, mixed, yt, skip, groups, block):
    row = pl.multiple_of(block * BLOCK, BLOCK)
    at = pl.multiple_of(block * GROUP_SIZE, GROUP_SIZE)
    parts = [yt[g, pl.ds(at, GROUP_SIZE), :] for g in range(groups)]
    if groups * GROUP_SIZE < LANES:
        parts.append(jnp.zeros((LANES - groups * GROUP_SIZE, BLOCK), jnp.float32))
    convolved = jnp.concatenate(parts, axis=0).T
    return gate[pl.ds(row, BLOCK), :].astype(jnp.float32) * (
        convolved + skip[...] * mixed[pl.ds(row, BLOCK), :].astype(jnp.float32)
    )


def operator_kernel(
    groups, blocks, holder, recv, reach, taps, skip, lags, out, gate, mixed, xt, yt, toep
):
    tiles = BLOCK // TILE
    for g in range(groups):
        xt[g, 0 : blocks * GROUP_SIZE, :] = jnp.zeros((blocks * GROUP_SIZE, BLOCK), xt.dtype)

    @pl.loop(0, blocks)
    def _(block):
        @pl.loop(0, tiles, unroll=4)
        def _(i):
            row, (q, k, v) = place_and_filter(
                holder, recv, reach, taps, (0, 1, 2), 0, block * tiles + i
            )
            gate[pl.ds(row, TILE), :] = q.astype(jnp.bfloat16)
            mixed[pl.ds(row, TILE), :] = (k * v).astype(jnp.bfloat16)

        to_columns(mixed, xt, groups, block, blocks)

    toeplitz(lags, toep, groups, blocks)
    long_conv(toep, xt, yt, groups, blocks)

    @pl.loop(0, blocks)
    def _(block):
        row = pl.multiple_of(block * BLOCK, BLOCK)
        out[pl.ds(row, BLOCK), :] = gate_block(gate, mixed, yt, skip, groups, block).astype(
            jnp.bfloat16
        )


def operator(holder, recv, reach, taps, skip, lags, groups):
    seq = reach.shape[0]
    blocks = seq // BLOCK
    vmem = pl.BlockSpec(memory_space=pltpu.VMEM)
    return pl.pallas_call(
        functools.partial(operator_kernel, groups, blocks),
        out_shape=jax.ShapeDtypeStruct((seq, LANES), jnp.bfloat16),
        in_specs=[pl.BlockSpec(memory_space=pltpu.SMEM)] + [vmem] * 5,
        out_specs=vmem,
        scratch_shapes=[
            pltpu.VMEM((seq, LANES), jnp.bfloat16),
            pltpu.VMEM((seq, LANES), jnp.bfloat16),
            pltpu.VMEM((groups, 2 * blocks * GROUP_SIZE, BLOCK), jnp.bfloat16),
            pltpu.VMEM((groups, blocks * GROUP_SIZE, BLOCK), jnp.float32),
            pltpu.VMEM((groups, LANES, seq + LANES), jnp.bfloat16),
        ],
        compiler_params=pltpu.CompilerParams(vmem_limit_bytes=62 * 2**20),
    )(holder, recv, reach, taps, skip, lags)


def exchange_kernel(
    blocks, axis_peers, holder, loaded, reach, taps, skip, filters, out,
    recv_q, recv_kv, mixed, xt, yt, toep, gated, lags,
    lag_send, lag_recv, kv_send, kv_recv, q_send, q_recv, back_send, back_recv, own_sem,
):
    devices = axis_peers
    me = lax.axis_index("seq")
    groups = LANES // GROUP_SIZE
    tiles = BLOCK // TILE
    seq_rows = blocks * BLOCK // devices
    per_device = seq_rows // BLOCK

    def peer_at(k):
        return lax.rem(me + k, devices)

    def lanes_of(index):
        return pl.ds(pl.multiple_of(index * LANES, LANES), LANES)

    filter_lags = filters.shape[1]

    def lag_rows(index):
        return filters.at[pl.ds(pl.multiple_of(index * groups, groups), groups), :]

    def lag_place():
        return lags.at[:, pl.ds(pl.multiple_of(LANES + me * filter_lags, LANES), filter_lags)]

    def lag_copy(k):
        return pltpu.make_async_remote_copy(
            src_ref=lag_rows(peer_at(k)),
            dst_ref=lag_place(),
            send_sem=lag_send.at[k],
            recv_sem=lag_recv.at[k],
            device_id={"seq": peer_at(k)},
            device_id_type=pl.DeviceIdType.MESH,
        )

    def kv_copy(k):
        return pltpu.make_async_remote_copy(
            src_ref=loaded.at[1:3, :, :, lanes_of(peer_at(k))],
            dst_ref=recv_kv.at[me],
            send_sem=kv_send.at[k],
            recv_sem=kv_recv.at[k],
            device_id={"seq": peer_at(k)},
            device_id_type=pl.DeviceIdType.MESH,
        )

    def q_copy(k):
        return pltpu.make_async_remote_copy(
            src_ref=loaded.at[0:1, :, :, lanes_of(peer_at(k))],
            dst_ref=recv_q.at[me],
            send_sem=q_send.at[k],
            recv_sem=q_recv.at[k],
            device_id={"seq": peer_at(k)},
            device_id_type=pl.DeviceIdType.MESH,
        )

    def rows_of(index):
        return pl.ds(pl.multiple_of(index * seq_rows, seq_rows), seq_rows)

    def back_copy(k):
        return pltpu.make_async_remote_copy(
            src_ref=gated.at[rows_of(peer_at(k))],
            dst_ref=out.at[:, lanes_of(me)],
            send_sem=back_send.at[k],
            recv_sem=back_recv.at[k],
            device_id={"seq": peer_at(k)},
            device_id_type=pl.DeviceIdType.MESH,
        )

    barrier = pltpu.get_barrier_semaphore()

    @pl.loop(1, devices)
    def _(k):
        pl.semaphore_signal(
            barrier, inc=1, device_id={"seq": peer_at(k)}, device_id_type=pl.DeviceIdType.MESH
        )

    pl.semaphore_wait(barrier, devices - 1)

    own_kv = pltpu.make_async_copy(
        loaded.at[1:3, :, :, lanes_of(me)], recv_kv.at[me], own_sem.at[0]
    )
    own_q = pltpu.make_async_copy(loaded.at[0:1, :, :, lanes_of(me)], recv_q.at[me], own_sem.at[1])
    own_back = pltpu.make_async_copy(gated.at[rows_of(me)], out.at[:, lanes_of(me)], own_sem.at[2])

    own_lag = pltpu.make_async_copy(lag_rows(me), lag_place(), own_sem.at[3])

    @pl.loop(1, devices)
    def _(k):
        lag_copy(k).start()

    @pl.loop(1, devices)
    def _(k):
        kv_copy(k).start()

    own_lag.start()
    own_kv.start()
    own_q.start()
    lags[:, 0:LANES] = jnp.zeros((groups, LANES), jnp.float32)
    own_lag.wait()

    @pl.loop(1, devices)
    def _(k):
        lag_copy(k).wait()

    toeplitz(lags, toep, groups, blocks)
    for g in range(groups):
        xt[g, 0 : blocks * GROUP_SIZE, :] = jnp.zeros((blocks * GROUP_SIZE, BLOCK), xt.dtype)

    @pl.loop(1, devices)
    def _(k):
        kv_copy(k).wait_send()
        q_copy(k).start()

    own_kv.wait()

    @pl.loop(1, devices)
    def _(k):
        kv_copy(k).wait_recv()

    @pl.loop(0, blocks)
    def _(block):
        @pl.loop(0, tiles, unroll=4)
        def _(i):
            row, (k, v) = place_and_filter(
                holder, recv_kv, reach, taps, (1, 2), 1, block * tiles + i
            )
            mixed[pl.ds(row, TILE), :] = (k * v).astype(jnp.bfloat16)

        to_columns(mixed, xt, groups, block, blocks)

    long_conv(toep, xt, yt, groups, blocks)

    own_q.wait()

    @pl.loop(1, devices)
    def _(k):
        q_copy(k).wait()

    def gate_rows_of(owner):
        for part in range(per_device):
            block = owner * per_device + part

            @pl.loop(0, tiles, unroll=4)
            def _(i):
                row, (q,) = place_and_filter(
                    holder, recv_q, reach, taps, (0,), 0, block * tiles + i
                )
                gated[pl.ds(row, TILE), :] = q.astype(jnp.bfloat16)

            row = pl.multiple_of(block * BLOCK, BLOCK)
            gated[pl.ds(row, BLOCK), :] = gate_block(
                gated, mixed, yt, skip, groups, block
            ).astype(jnp.bfloat16)

    @pl.loop(1, devices)
    def _(k):
        gate_rows_of(peer_at(k))
        back_copy(k).start()

    gate_rows_of(me)
    own_back.start()
    own_back.wait()

    @pl.loop(1, devices)
    def _(k):
        back_copy(k).wait()


def exchange_operator(holder, loaded, reach, taps, skip, filters, devices):
    seq = reach.shape[0]
    blocks = seq // BLOCK
    groups = LANES // GROUP_SIZE
    cap = loaded.shape[1]
    vmem = pl.BlockSpec(memory_space=pltpu.VMEM)
    anywhere = pl.BlockSpec(memory_space=pl.ANY)
    dma = pltpu.SemaphoreType.DMA
    return pl.pallas_call(
        functools.partial(exchange_kernel, blocks, devices),
        out_shape=jax.ShapeDtypeStruct((seq // devices, loaded.shape[3]), jnp.bfloat16),
        in_specs=[pl.BlockSpec(memory_space=pltpu.SMEM), anywhere] + [vmem] * 4,
        out_specs=anywhere,
        scratch_shapes=[
            pltpu.VMEM((devices, 1, cap, TILE, LANES), jnp.bfloat16),
            pltpu.VMEM((devices, 2, cap, TILE, LANES), jnp.bfloat16),
            pltpu.VMEM((seq, LANES), jnp.bfloat16),
            pltpu.VMEM((groups, 2 * blocks * GROUP_SIZE, BLOCK), jnp.bfloat16),
            pltpu.VMEM((groups, blocks * GROUP_SIZE, BLOCK), jnp.float32),
            pltpu.VMEM((groups, LANES, seq + LANES), jnp.bfloat16),
            pltpu.VMEM((seq, LANES), jnp.bfloat16),
            pltpu.VMEM((groups, seq + LANES), jnp.float32),
        ]
        + [dma((devices,))] * 8
        + [dma((4,))],
        compiler_params=pltpu.CompilerParams(
            vmem_limit_bytes=60 * 2**20, collective_id=0, has_side_effects=True
        ),
    )(holder, loaded, reach, taps, skip, filters)


def routing(dest_tiles, tile_counts, segments):
    cap = dest_tiles.shape[0]
    marked = jnp.where(jnp.arange(cap, dtype=jnp.int32) < tile_counts[0], dest_tiles, -1)
    devices = lax.axis_size("seq")
    ints = jnp.concatenate([segments, marked])
    copies = jnp.broadcast_to(ints, (devices, ints.shape[0]))
    gathered = lax.all_to_all(copies, "seq", split_axis=0, concat_axis=0, tiled=True)
    docs = gathered[:, : segments.shape[0]].reshape(-1)
    slots = gathered[:, segments.shape[0] :].reshape(-1)
    seq = docs.shape[0]
    ids = jnp.arange(slots.shape[0], dtype=jnp.int32)
    hits = slots[None, :] == jnp.arange(seq // TILE, dtype=jnp.int32)[:, None]
    holder = jnp.sum(jnp.where(hits, ids[None, :], 0), axis=1)
    reach = jnp.zeros((seq,), jnp.int32)
    for offset in range(1, 7):
        same = docs[offset:] == docs[: seq - offset]
        reach = reach + jnp.pad(same.astype(jnp.int32), (offset, 0))
    holder = jnp.stack([holder // cap, holder % cap])
    return holder, jnp.broadcast_to(reach.astype(jnp.bfloat16)[:, None], (seq, LANES))


def whole_filters(long_filters, devices, groups):
    count = long_filters.shape[0]
    if count < devices * groups:
        long_filters = jnp.repeat(long_filters, devices * groups // count, axis=0)
    mine = lax.all_to_all(long_filters, "seq", split_axis=0, concat_axis=1, tiled=True)
    return jnp.pad(mine.astype(jnp.float32), ((0, 0), (LANES, 0)))


def local(
    loaded, dest_tiles, tile_counts, segments, short_filters, long_filters, skip_gain, norm_gain
):
    devices = lax.axis_size("seq")
    chans_all = loaded.shape[2] * lax.axis_size("chan")
    chans_here = loaded.shape[2]
    width = chans_here // devices
    groups = max(1, width // GROUP_SIZE)
    rows = loaded.shape[1]
    cap = dest_tiles.shape[0]
    me = lax.axis_index("seq")
    pad = LANES - width
    holder, reach = routing(dest_tiles, tile_counts, segments)
    taps = lax.dynamic_slice_in_dim(short_filters, me * width, width, 2)
    taps = jnp.pad(taps, ((0, 0), (0, 1), (0, pad)))
    skip = jnp.pad(lax.dynamic_slice_in_dim(skip_gain, me * width, width, 0), (0, pad))[None, :]
    if width == LANES:
        filters = long_filters.astype(jnp.float32)
        tiled = loaded.reshape(3, cap, TILE, chans_here)
        arrived = exchange_operator(holder, tiled, reach, taps, skip, filters, devices)
    else:
        lags = whole_filters(long_filters, devices, groups)
        sliced = jnp.transpose(loaded.reshape(3, rows, devices, width), (2, 0, 1, 3))
        recv = lax.all_to_all(sliced, "seq", split_axis=0, concat_axis=0, tiled=True)
        recv = jnp.pad(recv, ((0, 0), (0, 0), (0, 0), (0, pad)))
        recv = recv.reshape(devices, 3, cap, TILE, LANES)
        gated = operator(holder, recv, reach, taps, skip, lags, groups)[:, :width]
        seq_rows = gated.shape[0] // devices
        back = lax.all_to_all(
            gated.reshape(devices, seq_rows, width), "seq", split_axis=0, concat_axis=0, tiled=True
        )
        arrived = jnp.transpose(back, (1, 0, 2)).reshape(seq_rows, chans_here)
    gated_rows = arrived.astype(jnp.float32)
    row_power = lax.psum(jnp.sum(gated_rows * gated_rows, axis=1), "chan") / chans_all
    return (gated_rows * lax.rsqrt(row_power + 1e-06)[:, None] * norm_gain[None, :]).astype(
        jnp.bfloat16
    )


def solution(mesh):
    return jax.shard_map(
        local,
        mesh=mesh,
        in_specs=(
            P(None, "seq", "chan"),
            P("seq"),
            P("seq"),
            P("seq"),
            P(None, None, "chan"),
            P("chan", "seq"),
            P("chan"),
            P("chan"),
        ),
        out_specs=P("seq", "chan"),
        check_vma=False,
    )
```

```python
import functools

import jax
import jax.numpy as jnp
from jax import lax
from jax.experimental import pallas as pl
from jax.experimental.pallas import tpu as pltpu
from jax.sharding import PartitionSpec as P

GROUP_SIZE = 16
TILE = 32
BLOCK = 256
LANES = 128
CHUNK = 1024


def place_and_filter(holder, recv, reach, taps, arrays, first, tile):
    back = jnp.maximum(tile - 1, 0)
    source, slot = holder[0, tile], holder[1, tile]
    back_source, back_slot = holder[0, back], holder[1, back]
    row = pl.multiple_of(tile * TILE, TILE)
    limit = reach[pl.ds(row, TILE), :].astype(jnp.float32)
    results = []
    for r in arrays:
        here = recv[source, r - first, slot, :, :].astype(jnp.float32)
        before = recv[back_source, r - first, back_slot, TILE // 2 :, :].astype(jnp.float32)
        ext = jnp.concatenate([before[TILE // 2 - 8 :], here], axis=0)
        total = here * taps[r, 0:1, :]
        for offset in range(1, 7):
            window = ext[8 - offset : 8 - offset + TILE]
            total = total + jnp.where(limit >= offset, window, 0.0) * taps[r, offset : offset + 1, :]
        results.append(total)
    return row, results


def toeplitz(lags, toep, groups, blocks):
    @pl.loop(0, groups)
    def _(g):
        toep[g, :, 0:LANES] = jnp.zeros((LANES, LANES), toep.dtype)

        @pl.loop(0, blocks * BLOCK // CHUNK)
        def _(c):
            base = pl.multiple_of(c * CHUNK, CHUNK)
            part = lags[pl.ds(g, 1), pl.ds(base, CHUNK + LANES)]
            part = jnp.broadcast_to(part, (LANES, CHUNK + LANES))
            rolled = pltpu.roll(part, 0, 1, stride=1, stride_axis=0)
            toep[g, :, pl.ds(base + LANES, CHUNK)] = rolled[:, LANES:].astype(toep.dtype)


def long_conv(toep, xt, yt, groups, blocks):
    @pl.loop(0, groups)
    def _(g):
        yt[g] = jnp.zeros((blocks * GROUP_SIZE, BLOCK), jnp.float32)
        stages = 4
        for stage in range(stages):
            first = stage * blocks // stages
            rows = (blocks - first) * GROUP_SIZE

            @pl.loop(first, first + blocks // stages)
            def _(d):
                begin = pl.multiple_of((blocks + first - d) * GROUP_SIZE, GROUP_SIZE)
                lag = pl.multiple_of(d * BLOCK, BLOCK)
                table = jnp.concatenate(
                    [toep[g, :, pl.ds(lag + LANES, BLOCK)], toep[g, :, pl.ds(lag, BLOCK)]], axis=0
                )
                yt[g, first * GROUP_SIZE :, :] += jnp.dot(
                    xt[g, pl.ds(begin, rows), :], table, preferred_element_type=jnp.float32
                )


def to_columns(mixed, xt, groups, block, blocks):
    row = pl.multiple_of(block * BLOCK, BLOCK)
    turned = mixed[pl.ds(row, BLOCK), :].astype(jnp.float32).T.astype(jnp.bfloat16)
    at = pl.multiple_of((blocks + block) * GROUP_SIZE, GROUP_SIZE)
    for g in range(groups):
        xt[g, pl.ds(at, GROUP_SIZE), :] = turned[g * GROUP_SIZE : (g + 1) * GROUP_SIZE]


def gate_block(gate, mixed, yt, skip, groups, block):
    row = pl.multiple_of(block * BLOCK, BLOCK)
    at = pl.multiple_of(block * GROUP_SIZE, GROUP_SIZE)
    parts = [yt[g, pl.ds(at, GROUP_SIZE), :] for g in range(groups)]
    if groups * GROUP_SIZE < LANES:
        parts.append(jnp.zeros((LANES - groups * GROUP_SIZE, BLOCK), jnp.float32))
    convolved = jnp.concatenate(parts, axis=0).T
    return gate[pl.ds(row, BLOCK), :].astype(jnp.float32) * (
        convolved + skip[...] * mixed[pl.ds(row, BLOCK), :].astype(jnp.float32)
    )


def operator_kernel(
    groups, blocks, holder, recv, reach, taps, skip, lags, out, gate, mixed, xt, yt, toep
):
    tiles = BLOCK // TILE
    for g in range(groups):
        xt[g, 0 : blocks * GROUP_SIZE, :] = jnp.zeros((blocks * GROUP_SIZE, BLOCK), xt.dtype)

    @pl.loop(0, blocks)
    def _(block):
        @pl.loop(0, tiles, unroll=4)
        def _(i):
            row, (q, k, v) = place_and_filter(
                holder, recv, reach, taps, (0, 1, 2), 0, block * tiles + i
            )
            gate[pl.ds(row, TILE), :] = q.astype(jnp.bfloat16)
            mixed[pl.ds(row, TILE), :] = (k * v).astype(jnp.bfloat16)

        to_columns(mixed, xt, groups, block, blocks)

    toeplitz(lags, toep, groups, blocks)
    long_conv(toep, xt, yt, groups, blocks)

    @pl.loop(0, blocks)
    def _(block):
        row = pl.multiple_of(block * BLOCK, BLOCK)
        out[pl.ds(row, BLOCK), :] = gate_block(gate, mixed, yt, skip, groups, block).astype(
            jnp.bfloat16
        )


def operator(holder, recv, reach, taps, skip, lags, groups):
    seq = reach.shape[0]
    blocks = seq // BLOCK
    vmem = pl.BlockSpec(memory_space=pltpu.VMEM)
    return pl.pallas_call(
        functools.partial(operator_kernel, groups, blocks),
        out_shape=jax.ShapeDtypeStruct((seq, LANES), jnp.bfloat16),
        in_specs=[pl.BlockSpec(memory_space=pltpu.SMEM)] + [vmem] * 5,
        out_specs=vmem,
        scratch_shapes=[
            pltpu.VMEM((seq, LANES), jnp.bfloat16),
            pltpu.VMEM((seq, LANES), jnp.bfloat16),
            pltpu.VMEM((groups, 2 * blocks * GROUP_SIZE, BLOCK), jnp.bfloat16),
            pltpu.VMEM((groups, blocks * GROUP_SIZE, BLOCK), jnp.float32),
            pltpu.VMEM((groups, LANES, seq + LANES), jnp.bfloat16),
        ],
        compiler_params=pltpu.CompilerParams(vmem_limit_bytes=62 * 2**20),
    )(holder, recv, reach, taps, skip, lags)


def exchange_kernel(
    blocks, axis_peers, holder, loaded, reach, taps, skip, filters, out,
    recv_q, recv_kv, mixed, xt, yt, toep, gated, lags,
    lag_send, lag_recv, kv_send, kv_recv, q_send, q_recv, back_send, back_recv, own_sem,
):
    devices = axis_peers
    me = lax.axis_index("seq")
    groups = LANES // GROUP_SIZE
    tiles = BLOCK // TILE
    seq_rows = blocks * BLOCK // devices
    per_device = seq_rows // BLOCK

    def peer_at(k):
        distance = devices // 2 + (k // 2) * (2 * (k % 2) - 1)
        return lax.rem(me + distance, devices)

    def lanes_of(index):
        return pl.ds(pl.multiple_of(index * LANES, LANES), LANES)

    filter_lags = filters.shape[1]

    def lag_rows(index):
        return filters.at[pl.ds(pl.multiple_of(index * groups, groups), groups), :]

    def lag_place():
        return lags.at[:, pl.ds(pl.multiple_of(LANES + me * filter_lags, LANES), filter_lags)]

    def lag_copy(k):
        return pltpu.make_async_remote_copy(
            src_ref=lag_rows(peer_at(k)),
            dst_ref=lag_place(),
            send_sem=lag_send.at[k],
            recv_sem=lag_recv.at[k],
            device_id={"seq": peer_at(k)},
            device_id_type=pl.DeviceIdType.MESH,
        )

    def kv_copy(k):
        return pltpu.make_async_remote_copy(
            src_ref=loaded.at[1:3, :, :, lanes_of(peer_at(k))],
            dst_ref=recv_kv.at[me],
            send_sem=kv_send.at[k],
            recv_sem=kv_recv.at[k],
            device_id={"seq": peer_at(k)},
            device_id_type=pl.DeviceIdType.MESH,
        )

    def q_copy(k):
        return pltpu.make_async_remote_copy(
            src_ref=loaded.at[0:1, :, :, lanes_of(peer_at(k))],
            dst_ref=recv_q.at[me],
            send_sem=q_send.at[k],
            recv_sem=q_recv.at[k],
            device_id={"seq": peer_at(k)},
            device_id_type=pl.DeviceIdType.MESH,
        )

    def rows_of(index):
        return pl.ds(pl.multiple_of(index * seq_rows, seq_rows), seq_rows)

    def back_copy(k):
        return pltpu.make_async_remote_copy(
            src_ref=gated.at[rows_of(peer_at(k))],
            dst_ref=out.at[:, lanes_of(me)],
            send_sem=back_send.at[k],
            recv_sem=back_recv.at[k],
            device_id={"seq": peer_at(k)},
            device_id_type=pl.DeviceIdType.MESH,
        )

    barrier = pltpu.get_barrier_semaphore()

    @pl.loop(1, devices)
    def _(k):
        pl.semaphore_signal(
            barrier, inc=1, device_id={"seq": peer_at(k)}, device_id_type=pl.DeviceIdType.MESH
        )

    pl.semaphore_wait(barrier, devices - 1)

    own_kv = pltpu.make_async_copy(
        loaded.at[1:3, :, :, lanes_of(me)], recv_kv.at[me], own_sem.at[0]
    )
    own_q = pltpu.make_async_copy(loaded.at[0:1, :, :, lanes_of(me)], recv_q.at[me], own_sem.at[1])
    own_back = pltpu.make_async_copy(gated.at[rows_of(me)], out.at[:, lanes_of(me)], own_sem.at[2])

    own_lag = pltpu.make_async_copy(lag_rows(me), lag_place(), own_sem.at[3])

    @pl.loop(1, devices)
    def _(k):
        lag_copy(k).start()

    @pl.loop(1, devices)
    def _(k):
        kv_copy(k).start()

    own_lag.start()
    own_kv.start()
    own_q.start()
    lags[:, 0:LANES] = jnp.zeros((groups, LANES), jnp.float32)
    own_lag.wait()

    @pl.loop(1, devices)
    def _(k):
        lag_copy(k).wait()

    toeplitz(lags, toep, groups, blocks)
    for g in range(groups):
        xt[g, 0 : blocks * GROUP_SIZE, :] = jnp.zeros((blocks * GROUP_SIZE, BLOCK), xt.dtype)

    @pl.loop(1, devices)
    def _(k):
        kv_copy(k).wait_send()
        q_copy(k).start()

    own_kv.wait()

    @pl.loop(1, devices)
    def _(k):
        kv_copy(k).wait_recv()

    @pl.loop(0, blocks)
    def _(block):
        @pl.loop(0, tiles, unroll=4)
        def _(i):
            row, (k, v) = place_and_filter(
                holder, recv_kv, reach, taps, (1, 2), 1, block * tiles + i
            )
            mixed[pl.ds(row, TILE), :] = (k * v).astype(jnp.bfloat16)

        to_columns(mixed, xt, groups, block, blocks)

    long_conv(toep, xt, yt, groups, blocks)

    own_q.wait()

    @pl.loop(1, devices)
    def _(k):
        q_copy(k).wait()

    def gate_rows_of(owner):
        for part in range(per_device):
            block = owner * per_device + part

            @pl.loop(0, tiles, unroll=4)
            def _(i):
                row, (q,) = place_and_filter(
                    holder, recv_q, reach, taps, (0,), 0, block * tiles + i
                )
                gated[pl.ds(row, TILE), :] = q.astype(jnp.bfloat16)

            row = pl.multiple_of(block * BLOCK, BLOCK)
            gated[pl.ds(row, BLOCK), :] = gate_block(
                gated, mixed, yt, skip, groups, block
            ).astype(jnp.bfloat16)

    @pl.loop(1, devices)
    def _(k):
        gate_rows_of(peer_at(k))
        back_copy(k).start()

    gate_rows_of(me)
    own_back.start()
    own_back.wait()

    @pl.loop(1, devices)
    def _(k):
        back_copy(k).wait()


def exchange_operator(holder, loaded, reach, taps, skip, filters, devices):
    seq = reach.shape[0]
    blocks = seq // BLOCK
    groups = LANES // GROUP_SIZE
    cap = loaded.shape[1]
    vmem = pl.BlockSpec(memory_space=pltpu.VMEM)
    anywhere = pl.BlockSpec(memory_space=pl.ANY)
    dma = pltpu.SemaphoreType.DMA
    return pl.pallas_call(
        functools.partial(exchange_kernel, blocks, devices),
        out_shape=jax.ShapeDtypeStruct((seq // devices, loaded.shape[3]), jnp.bfloat16),
        in_specs=[pl.BlockSpec(memory_space=pltpu.SMEM), anywhere] + [vmem] * 4,
        out_specs=anywhere,
        scratch_shapes=[
            pltpu.VMEM((devices, 1, cap, TILE, LANES), jnp.bfloat16),
            pltpu.VMEM((devices, 2, cap, TILE, LANES), jnp.bfloat16),
            pltpu.VMEM((seq, LANES), jnp.bfloat16),
            pltpu.VMEM((groups, 2 * blocks * GROUP_SIZE, BLOCK), jnp.bfloat16),
            pltpu.VMEM((groups, blocks * GROUP_SIZE, BLOCK), jnp.float32),
            pltpu.VMEM((groups, LANES, seq + LANES), jnp.bfloat16),
            pltpu.VMEM((seq, LANES), jnp.bfloat16),
            pltpu.VMEM((groups, seq + LANES), jnp.float32),
        ]
        + [dma((devices,))] * 8
        + [dma((4,))],
        compiler_params=pltpu.CompilerParams(
            vmem_limit_bytes=60 * 2**20, collective_id=0, has_side_effects=True
        ),
    )(holder, loaded, reach, taps, skip, filters)


def routing(dest_tiles, tile_counts, segments):
    cap = dest_tiles.shape[0]
    marked = jnp.where(jnp.arange(cap, dtype=jnp.int32) < tile_counts[0], dest_tiles, -1)
    devices = lax.axis_size("seq")
    ints = jnp.concatenate([segments, marked])
    copies = jnp.broadcast_to(ints, (devices, ints.shape[0]))
    gathered = lax.all_to_all(copies, "seq", split_axis=0, concat_axis=0, tiled=True)
    docs = gathered[:, : segments.shape[0]].reshape(-1)
    slots = gathered[:, segments.shape[0] :].reshape(-1)
    seq = docs.shape[0]
    ids = jnp.arange(slots.shape[0], dtype=jnp.int32)
    hits = slots[None, :] == jnp.arange(seq // TILE, dtype=jnp.int32)[:, None]
    holder = jnp.sum(jnp.where(hits, ids[None, :], 0), axis=1)
    reach = jnp.zeros((seq,), jnp.int32)
    for offset in range(1, 7):
        same = docs[offset:] == docs[: seq - offset]
        reach = reach + jnp.pad(same.astype(jnp.int32), (offset, 0))
    holder = jnp.stack([holder // cap, holder % cap])
    return holder, jnp.broadcast_to(reach.astype(jnp.bfloat16)[:, None], (seq, LANES))


def whole_filters(long_filters, devices, groups):
    count = long_filters.shape[0]
    if count < devices * groups:
        long_filters = jnp.repeat(long_filters, devices * groups // count, axis=0)
    mine = lax.all_to_all(long_filters, "seq", split_axis=0, concat_axis=1, tiled=True)
    return jnp.pad(mine.astype(jnp.float32), ((0, 0), (LANES, 0)))


def local(
    loaded, dest_tiles, tile_counts, segments, short_filters, long_filters, skip_gain, norm_gain
):
    devices = lax.axis_size("seq")
    chans_all = loaded.shape[2] * lax.axis_size("chan")
    chans_here = loaded.shape[2]
    width = chans_here // devices
    groups = max(1, width // GROUP_SIZE)
    rows = loaded.shape[1]
    cap = dest_tiles.shape[0]
    me = lax.axis_index("seq")
    pad = LANES - width
    holder, reach = routing(dest_tiles, tile_counts, segments)
    taps = lax.dynamic_slice_in_dim(short_filters, me * width, width, 2)
    taps = jnp.pad(taps, ((0, 0), (0, 1), (0, pad)))
    skip = jnp.pad(lax.dynamic_slice_in_dim(skip_gain, me * width, width, 0), (0, pad))[None, :]
    if width == LANES:
        filters = long_filters.astype(jnp.float32)
        tiled = loaded.reshape(3, cap, TILE, chans_here)
        arrived = exchange_operator(holder, tiled, reach, taps, skip, filters, devices)
    else:
        lags = whole_filters(long_filters, devices, groups)
        sliced = jnp.transpose(loaded.reshape(3, rows, devices, width), (2, 0, 1, 3))
        recv = lax.all_to_all(sliced, "seq", split_axis=0, concat_axis=0, tiled=True)
        recv = jnp.pad(recv, ((0, 0), (0, 0), (0, 0), (0, pad)))
        recv = recv.reshape(devices, 3, cap, TILE, LANES)
        gated = operator(holder, recv, reach, taps, skip, lags, groups)[:, :width]
        seq_rows = gated.shape[0] // devices
        back = lax.all_to_all(
            gated.reshape(devices, seq_rows, width), "seq", split_axis=0, concat_axis=0, tiled=True
        )
        arrived = jnp.transpose(back, (1, 0, 2)).reshape(seq_rows, chans_here)
    gated_rows = arrived.astype(jnp.float32)
    row_power = lax.psum(jnp.sum(gated_rows * gated_rows, axis=1), "chan") / chans_all
    return (gated_rows * lax.rsqrt(row_power + 1e-06)[:, None] * norm_gain[None, :]).astype(
        jnp.bfloat16
    )


def solution(mesh):
    return jax.shard_map(
        local,
        mesh=mesh,
        in_specs=(
            P(None, "seq", "chan"),
            P("seq"),
            P("seq"),
            P("seq"),
            P(None, None, "chan"),
            P("chan", "seq"),
            P("chan"),
            P("chan"),
        ),
        out_specs=P("seq", "chan"),
        check_vma=False,
    )
```
